128 devices in a mesh: row: 8 (over y_lo, z), col: 16 (over x, y_hi, core).
Axes of the slice: x: 4, y: 4 (y_hi: 2, y_lo: 2; y = y_hi * 2 + y_lo), z: 4, core: 2. Of those that a mesh axis runs over, the one named last changes fastest.
Arguments:
- amplitudes: float32 [512, 20480], P('row', 'col'), may hold values from -6 to 6
- integrals: float32 [512, 38400], P('col', 'row'), may hold values from -0.25 to 0.25
Outputs:
- residual: float32 [38400, 20480], P('row', 'col')
The draws below stay inside these ranges and needn't reach their ends.
All inputs are finite; a program needn't handle non-finite values.
Results may differ from the reference program's by a relative error of at most 0.00007.
Values sent between devices are 32-bit elements; how exact they have to be, the bound alone decides.
No kernel may reach another device: no remote copies, remote signals or barrier semaphores. Data moves between devices by JAX's collectives and lax.ppermute only.
A program may use at most 128 MiB of HBM per device.

```python
import jax
import jax.numpy as jnp
from jax import lax

CD = 512
AB = 38400
PAIRS = 20480


def block_scale(own_key, shape, shards, low, high):
    def one(position, blocks):
        steps = jax.random.uniform(jax.random.fold_in(jax.random.fold_in(own_key, 6), position), (blocks,), jnp.float32, low / len(shards), high / len(shards))
        return jnp.repeat(jnp.exp(steps), shape[position] // blocks).reshape((-1,) + (1,) * (len(shape) - position - 1))

    level = one(*shards[0])
    for cut in shards[1:]:
        level = level * one(*cut)
    return level


def normal_values(key, dims, scale, limit, shards=(), held_as=jnp.bfloat16):
    values = scale * jax.random.normal(key, dims, jnp.float32)
    if shards:
        values = values * block_scale(key, dims, shards, -0.22, 0.18)
    return jnp.clip(values, -limit, limit).astype(held_as)


def setup_inputs(seed: int = 0) -> dict:
    seeds = jax.random.split(jax.random.key(seed), 3)
    amplitudes = normal_values(seeds[0], (CD, PAIRS), 1.0, 6.0, ((0, 8), (1, 16)), jnp.float32)
    integrals = normal_values(seeds[1], (CD, AB), CD ** -0.5, 0.25, ((0, 16), (1, 8)), jnp.float32)
    return dict(amplitudes=amplitudes, integrals=integrals)


def reference(amplitudes, integrals):
    ladder = lax.dot_general(integrals, amplitudes, (((0,), (0,)), ((), ())), precision=lax.Precision.HIGHEST, preferred_element_type=jnp.float32)
    return 0.5 * ladder
```

```python
import jax
import jax.numpy as jnp
from jax import lax
from jax.experimental import pallas as pl
from jax.experimental.pallas import tpu as pltpu
from jax.sharding import PartitionSpec as P

NZ, NX = 4, 4
BF, F32 = jnp.bfloat16, jnp.float32
WIDE = 1280
CHUNKS = ((1280, 1280, 320), (2560, 1280, 320), (3840, 960, 240))
EARLY = False
CUT_AT = 1


def swap_core(v):
    return lax.ppermute(v, "col", [(i, i ^ 1) for i in range(16)])


def swap_y_hi(v):
    return lax.ppermute(v, "col", [(i, i ^ 2) for i in range(16)])


def swap_y_lo(v):
    return lax.ppermute(v, "row", [(i, i ^ 4) for i in range(8)])


def shift_x(v):
    return lax.ppermute(v, "col", [(i, (i + (4 if i % 2 == 0 else 12)) % 16) for i in range(16)])


def send_x(v, d):
    return lax.ppermute(v, "col", [(i, (i + 4 * d) % 16) for i in range(16)])


def shift_z(v):
    pairs = []
    for row in range(8):
        for col in range(16):
            z = (row % 4 + (1 if col % 2 == 0 else 3)) % 4
            pairs.append((row * 16 + col, (row // 4 * 4 + z) * 16 + col))
    return lax.ppermute(v, ("row", "col"), pairs)


def tie(value, done):
    return lax.optimization_barrier((value, done))


def split(v):
    high = v.astype(BF)
    return high, (v - high.astype(F32)).astype(BF)


def amps_kernel(own, near, far, opposite, y_own, y_near, y_far, y_opposite, out):
    row, col = lax.axis_index("row"), lax.axis_index("col")
    y_lo, z = row // NZ, row % NZ
    x, step = col // 4, 1 - 2 * (col % 2)
    sides = ((y_lo, own, near, far, opposite), (1 - y_lo, y_own, y_near, y_far, y_opposite))
    for y, *pieces in sides:
        for piece, zz in zip(pieces, (z, z - step, z + step, z + 2)):
            high, low = split(piece[...] * 0.5)
            zz = (zz + NZ) % NZ
            slot = ((y * 2 + zz // 2 - x) * step + 2 * NX) % NX
            at = pl.multiple_of(slot * 128 + zz % 2 * 64, 64)
            out[pl.ds(at, 64), :] = high
            out[pl.ds(at + 512, 64), :] = high
            out[pl.ds(at + 1024, 64), :] = low


def stack_amps(pieces):
    pairs = pieces[0].shape[1]
    return pl.pallas_call(
        amps_kernel,
        grid=(pairs // 256,),
        out_shape=jax.ShapeDtypeStruct((1536, pairs), BF),
        in_specs=[pl.BlockSpec((64, 256), lambda i: (0, i))] * 8,
        out_specs=pl.BlockSpec((1536, 256), lambda i: (0, i)),
        compiler_params=pltpu.CompilerParams(vmem_limit_bytes=8 << 20),
        cost_estimate=pl.CostEstimate(flops=3 << 20, bytes_accessed=6 << 20, transcendentals=0),
    )(*pieces)


def turn_kernel(own, other, y_own, y_other, first, second, rows):
    col = lax.axis_index("col")
    place, core = col % 4, col % 2
    for piece, p in ((own, place), (other, place ^ 1), (y_own, place ^ 2), (y_other, place ^ 3)):
        rows[pl.ds(pl.multiple_of(p * 32, 32), 32), :] = piece[...]
    n = first.shape[0]
    tall = rows[...].T
    top, bottom = tall[:n], tall[n : 2 * n]
    first[...] = jnp.where(core == 0, top, bottom)
    second[...] = jnp.where(core == 0, bottom, top)


def turn(start, width, own, other, y_own, y_other, y_start):
    def part(first):
        return pl.BlockSpec((32, WIDE), lambda i: (0, first // WIDE))

    half = jax.ShapeDtypeStruct((width // 2, 128), F32)
    return pl.pallas_call(
        turn_kernel,
        grid=(1,),
        out_shape=[half, half],
        in_specs=[part(start)] * 2 + [part(y_start)] * 2,
        out_specs=[pl.BlockSpec((width // 2, 128), lambda i: (0, 0))] * 2,
        scratch_shapes=[pltpu.VMEM((128, WIDE), F32)],
        compiler_params=pltpu.CompilerParams(vmem_limit_bytes=8 << 20),
        cost_estimate=pl.CostEstimate(flops=1 << 20, bytes_accessed=2 << 20, transcendentals=0),
    )(own, other, y_own, y_other)


def product_kernel(own, far, opposite, near, own2, far2, opposite2, near2, amps, *rest):
    out, left = rest[-2:]
    steps = pl.num_programs(0) // 2

    def run(pieces):
        for k, piece in enumerate(pieces):
            high, low = split(piece[...])
            left[:, k * 128 : k * 128 + 128] = high
            left[:, k * 128 + 512 : k * 128 + 640] = low
            left[:, k * 128 + 1024 : k * 128 + 1152] = high
        out[...] = jnp.dot(left[...], amps[...], preferred_element_type=F32)

    @pl.when(pl.program_id(0) < steps)
    def _():
        run((own, far, opposite, near))

    @pl.when(pl.program_id(0) >= steps)
    def _():
        run((own2, far2, opposite2, near2))


def cut_kernel(own, other, right, left_, far, right_o, left_o, far_o, y, y_o, amps, *rest):
    out, rows, left = rest[-3:]
    col = lax.axis_index("col")
    y_hi, core = col // 2 % 2, col % 2

    def put(value, slot, y_side, c):
        rows[pl.ds(pl.multiple_of(slot * 128 + y_side * 64 + c * 32, 32), 32), :] = value

    from_left = jnp.where(core == 0, 3, 1)
    from_right = jnp.where(core == 0, 1, 3)
    for c, parts in ((core, (own, right, left_, far)), (1 - core, (other, right_o, left_o, far_o))):
        for part, slot in zip(parts, (0, from_left, from_right, 2)):
            put(part[...], slot, y_hi, c)
    for c, part in ((core, y), (1 - core, y_o)):
        for k, slot in enumerate((0, from_left, from_right, 2)):
            put(part[k * 32 : k * 32 + 32], slot, 1 - y_hi, c)
    high, low = split(rows[...].T)
    left[:, :512] = high
    left[:, 512:1024] = low
    left[:, 1024:] = high
    out[...] = jnp.dot(left[...], amps[...], preferred_element_type=F32)


def product_cut(pieces, amps, shape, before):
    in_specs = [pl.BlockSpec((min(p.shape[0], 128), 256), lambda i: (0, i)) for p in pieces]
    in_specs.append(pl.BlockSpec(memory_space=pltpu.VMEM))
    operands = [*pieces, amps]
    aliases = {}
    if before is not None:
        aliases = {len(operands): 0}
        in_specs.append(pl.BlockSpec(memory_space=pl.ANY))
        operands.append(before)
    return pl.pallas_call(
        cut_kernel,
        grid=(WIDE // 256,),
        out_shape=jax.ShapeDtypeStruct(shape, F32),
        in_specs=in_specs,
        out_specs=pl.BlockSpec((256, shape[1]), lambda i: (i, 0)),
        scratch_shapes=[pltpu.VMEM((512, 256), F32), pltpu.VMEM((256, 1536), BF)],
        input_output_aliases=aliases,
        compiler_params=pltpu.CompilerParams(vmem_limit_bytes=20 << 20),
        cost_estimate=pl.CostEstimate(flops=2 * WIDE * 1536 * shape[1], bytes_accessed=4 * WIDE * shape[1], transcendentals=0),
    )(*operands)


def product(start, width, tile, pieces, amps, shape, before):
    first, steps = start // tile, width // tile

    def rows(i):
        core = lax.axis_index("col") % 2
        return first + (i + core * (steps // 2)) % steps, 0

    in_specs = [pl.BlockSpec((tile, 128), lambda i: (jnp.minimum(i, steps // 2 - 1), 0))] * 4
    in_specs += [pl.BlockSpec((tile, 128), lambda i: (jnp.maximum(i - steps // 2, 0), 0))] * 4
    in_specs.append(pl.BlockSpec(memory_space=pltpu.VMEM))
    operands = [*pieces, amps]
    aliases = {}
    if before is not None:
        aliases = {len(operands): 0}
        in_specs.append(pl.BlockSpec(memory_space=pl.ANY))
        operands.append(before)
    return pl.pallas_call(
        product_kernel,
        grid=(steps,),
        out_shape=jax.ShapeDtypeStruct(shape, F32),
        in_specs=in_specs,
        out_specs=pl.BlockSpec((tile, shape[1]), rows),
        scratch_shapes=[pltpu.VMEM((tile, 1536), BF)],
        input_output_aliases=aliases,
        compiler_params=pltpu.CompilerParams(vmem_limit_bytes=20 << 20),
        cost_estimate=pl.CostEstimate(flops=2 * width * 1536 * shape[1], bytes_accessed=4 * width * shape[1], transcendentals=0),
    )(*operands)


def body(amplitudes, integrals):
    shape = (integrals.shape[1], amplitudes.shape[1])
    v, a = integrals, amplitudes
    ao, za, ya = swap_core(a), shift_z(a), swap_y_lo(a)
    zb, zy, yo = shift_z(ao), shift_z(ya), swap_core(ya)
    z2, y2, zz, zf = shift_z(za), shift_z(zy), shift_z(yo), swap_core(zb)
    zg = swap_core(zz)
    amps_in = (a, za, zf, z2, ya, zy, zg, y2)
    other = swap_core(v)
    v_cut, v0, rest = v[:, :WIDE], v[:, WIDE : 2 * WIDE], v[:, 2 * WIDE :]
    y0, y1 = swap_y_hi(v0), swap_y_hi(rest)
    cut = [send_x(v_cut, 1), send_x(v_cut, -1), send_x(v_cut, 2)]
    y_cut = swap_y_hi(jnp.concatenate([v_cut, *cut], 0))
    t0 = turn(WIDE, 1280, v, other, y0, swap_core(y0), 0)
    y1_other = swap_core(y1)
    t1, t2 = [turn(s, w, v, other, y1, y1_other, s - 2 * WIDE) for s, w, _ in CHUNKS[1:]]
    near0 = [shift_x(t) for t in t0]
    o0 = shift_x(near0[0])
    near1 = [shift_x(t) for t in t1] if EARLY else None
    amps_in, cut, y_cut, near0, o0, near1, t1, t2 = lax.optimization_barrier((amps_in, cut, y_cut, near0, o0, near1, t1, t2))
    if not EARLY:
        near1 = [shift_x(t) for t in t1]
    amps = stack_amps(amps_in)
    near2 = [shift_x(t) for t in t2]
    o1 = shift_x(near1[0])
    o2 = shift_x(near2[0])
    work = [(t0, near0, o0), (t1, near1, o1), (t2, near2, o2)]
    out = None
    for j, (start, width, tile) in enumerate(CHUNKS):
        if j == CUT_AT:
            cut_other = [swap_core(p) for p in cut]
            out = product_cut((v, other, *cut, *cut_other, y_cut, swap_core(y_cut)), amps, shape, out)
        (f, s), (near_f, near_s), o = work[j]
        pieces = (f, swap_core(near_s), o, near_f, s, swap_core(near_f), swap_core(o), near_s)
        out = product(start, width, tile, pieces, amps, shape, out)
    return out


def solution(mesh):
    in_specs = (P("row", "col"), P("col", "row"))
    out_specs = P("row", "col")
    return jax.shard_map(body, mesh=mesh, in_specs=in_specs, out_specs=out_specs, check_vma=False)
```

```python
import jax
import jax.numpy as jnp
from jax import lax
from jax.experimental import pallas as pl
from jax.experimental.pallas import tpu as pltpu
from jax.sharding import PartitionSpec as P

NZ, NX = 4, 4
BF, F32 = jnp.bfloat16, jnp.float32
WIDE = 1280
CHUNKS = ((1280, 1280, 320), (2560, 1280, 320), (3840, 960, 240))
EARLY = False
CUT_AT = 1


def swap_core(v):
    return lax.ppermute(v, "col", [(i, i ^ 1) for i in range(16)])


def swap_y_hi(v):
    return lax.ppermute(v, "col", [(i, i ^ 2) for i in range(16)])


def swap_y_lo(v):
    return lax.ppermute(v, "row", [(i, i ^ 4) for i in range(8)])


def shift_x(v):
    return lax.ppermute(v, "col", [(i, (i + (4 if i % 2 == 0 else 12)) % 16) for i in range(16)])


def send_x(v, d):
    return lax.ppermute(v, "col", [(i, (i + 4 * d) % 16) for i in range(16)])


def shift_z(v):
    pairs = []
    for row in range(8):
        for col in range(16):
            z = (row % 4 + (1 if col % 2 == 0 else 3)) % 4
            pairs.append((row * 16 + col, (row // 4 * 4 + z) * 16 + col))
    return lax.ppermute(v, ("row", "col"), pairs)


def tie(value, done):
    return lax.optimization_barrier((value, done))


def split(v):
    high = v.astype(BF)
    return high, (v - high.astype(F32)).astype(BF)


def amps_kernel(own, near, far, opposite, y_own, y_near, y_far, y_opposite, out):
    row, col = lax.axis_index("row"), lax.axis_index("col")
    y_lo, z = row // NZ, row % NZ
    x, step = col // 4, 1 - 2 * (col % 2)
    sides = ((y_lo, own, near, far, opposite), (1 - y_lo, y_own, y_near, y_far, y_opposite))
    for y, *pieces in sides:
        for piece, zz in zip(pieces, (z, z - step, z + step, z + 2)):
            high, low = split(piece[...] * 0.5)
            zz = (zz + NZ) % NZ
            slot = ((y * 2 + zz // 2 - x) * step + 2 * NX) % NX
            at = pl.multiple_of(slot * 128 + zz % 2 * 64, 64)
            out[pl.ds(at, 64), :] = high
            out[pl.ds(at + 512, 64), :] = high
            out[pl.ds(at + 1024, 64), :] = low


def stack_amps(pieces):
    pairs = pieces[0].shape[1]
    return pl.pallas_call(
        amps_kernel,
        grid=(pairs // 256,),
        out_shape=jax.ShapeDtypeStruct((1536, pairs), BF),
        in_specs=[pl.BlockSpec((64, 256), lambda i: (0, i))] * 8,
        out_specs=pl.BlockSpec((1536, 256), lambda i: (0, i)),
        compiler_params=pltpu.CompilerParams(vmem_limit_bytes=8 << 20),
        cost_estimate=pl.CostEstimate(flops=3 << 20, bytes_accessed=6 << 20, transcendentals=0),
    )(*pieces)


def turn_kernel(own, other, y_own, y_other, first, second, rows):
    col = lax.axis_index("col")
    place, core = col % 4, col % 2
    for piece, p in ((own, place), (other, place ^ 1), (y_own, place ^ 2), (y_other, place ^ 3)):
        rows[pl.ds(pl.multiple_of(p * 32, 32), 32), :] = piece[...]
    n = first.shape[0]
    tall = rows[...].T
    top, bottom = tall[:n], tall[n : 2 * n]
    first[...] = jnp.where(core == 0, top, bottom)
    second[...] = jnp.where(core == 0, bottom, top)


def turn(start, width, own, other, y_own, y_other, y_start):
    def part(first):
        return pl.BlockSpec((32, WIDE), lambda i: (0, first // WIDE))

    half = jax.ShapeDtypeStruct((width // 2, 128), F32)
    return pl.pallas_call(
        turn_kernel,
        grid=(1,),
        out_shape=[half, half],
        in_specs=[part(start)] * 2 + [part(y_start)] * 2,
        out_specs=[pl.BlockSpec((width // 2, 128), lambda i: (0, 0))] * 2,
        scratch_shapes=[pltpu.VMEM((128, WIDE), F32)],
        compiler_params=pltpu.CompilerParams(vmem_limit_bytes=8 << 20),
        cost_estimate=pl.CostEstimate(flops=1 << 20, bytes_accessed=2 << 20, transcendentals=0),
    )(own, other, y_own, y_other)


def product_kernel(own, far, opposite, near, own2, far2, opposite2, near2, amps, *rest):
    out, left = rest[-2:]
    steps = pl.num_programs(0) // 2

    def run(pieces):
        for k, piece in enumerate(pieces):
            high, low = split(piece[...])
            left[:, k * 128 : k * 128 + 128] = high
            left[:, k * 128 + 512 : k * 128 + 640] = low
            left[:, k * 128 + 1024 : k * 128 + 1152] = high
        out[...] = jnp.dot(left[...], amps[...], preferred_element_type=F32)

    @pl.when(pl.program_id(0) < steps)
    def _():
        run((own, far, opposite, near))

    @pl.when(pl.program_id(0) >= steps)
    def _():
        run((own2, far2, opposite2, near2))


def cut_kernel(mine, others, y_mine, y_others, amps, *rest):
    out, rows, left = rest[-3:]
    col = lax.axis_index("col")
    y_hi, core = col // 2 % 2, col % 2
    slots = (0, jnp.where(core == 0, 3, 1), jnp.where(core == 0, 1, 3), 2)
    for y_side, c, part in ((y_hi, core, mine), (y_hi, 1 - core, others), (1 - y_hi, core, y_mine), (1 - y_hi, 1 - core, y_others)):
        for k, slot in enumerate(slots):
            at = pl.multiple_of(slot * 128 + y_side * 64 + c * 32, 32)
            rows[pl.ds(at, 32), :] = part[k * 32 : k * 32 + 32]
    high, low = split(rows[...].T)
    left[:, :512] = high
    left[:, 512:1024] = low
    left[:, 1024:] = high
    out[...] = jnp.dot(left[...], amps[...], preferred_element_type=F32)


def product_cut(pieces, amps, shape, before):
    in_specs = [pl.BlockSpec((min(p.shape[0], 128), 256), lambda i: (0, i)) for p in pieces]
    in_specs.append(pl.BlockSpec(memory_space=pltpu.VMEM))
    operands = [*pieces, amps]
    aliases = {}
    if before is not None:
        aliases = {len(operands): 0}
        in_specs.append(pl.BlockSpec(memory_space=pl.ANY))
        operands.append(before)
    return pl.pallas_call(
        cut_kernel,
        grid=(WIDE // 256,),
        out_shape=jax.ShapeDtypeStruct(shape, F32),
        in_specs=in_specs,
        out_specs=pl.BlockSpec((256, shape[1]), lambda i: (i, 0)),
        scratch_shapes=[pltpu.VMEM((512, 256), F32), pltpu.VMEM((256, 1536), BF)],
        input_output_aliases=aliases,
        compiler_params=pltpu.CompilerParams(vmem_limit_bytes=20 << 20),
        cost_estimate=pl.CostEstimate(flops=2 * WIDE * 1536 * shape[1], bytes_accessed=4 * WIDE * shape[1], transcendentals=0),
    )(*operands)


def product(start, width, tile, pieces, amps, shape, before):
    first, steps = start // tile, width // tile

    def rows(i):
        core = lax.axis_index("col") % 2
        return first + (i + core * (steps // 2)) % steps, 0

    in_specs = [pl.BlockSpec((tile, 128), lambda i: (jnp.minimum(i, steps // 2 - 1), 0))] * 4
    in_specs += [pl.BlockSpec((tile, 128), lambda i: (jnp.maximum(i - steps // 2, 0), 0))] * 4
    in_specs.append(pl.BlockSpec(memory_space=pltpu.VMEM))
    operands = [*pieces, amps]
    aliases = {}
    if before is not None:
        aliases = {len(operands): 0}
        in_specs.append(pl.BlockSpec(memory_space=pl.ANY))
        operands.append(before)
    return pl.pallas_call(
        product_kernel,
        grid=(steps,),
        out_shape=jax.ShapeDtypeStruct(shape, F32),
        in_specs=in_specs,
        out_specs=pl.BlockSpec((tile, shape[1]), rows),
        scratch_shapes=[pltpu.VMEM((tile, 1536), BF)],
        input_output_aliases=aliases,
        compiler_params=pltpu.CompilerParams(vmem_limit_bytes=20 << 20),
        cost_estimate=pl.CostEstimate(flops=2 * width * 1536 * shape[1], bytes_accessed=4 * width * shape[1], transcendentals=0),
    )(*operands)


def body(amplitudes, integrals):
    shape = (integrals.shape[1], amplitudes.shape[1])
    v, a = integrals, amplitudes
    ao, za, ya = swap_core(a), shift_z(a), swap_y_lo(a)
    zb, zy, yo = shift_z(ao), shift_z(ya), swap_core(ya)
    z2, y2, zz, zf = shift_z(za), shift_z(zy), shift_z(yo), swap_core(zb)
    zg = swap_core(zz)
    amps_in = (a, za, zf, z2, ya, zy, zg, y2)
    other = swap_core(v)
    v_cut, v0, rest = v[:, :WIDE], v[:, WIDE : 2 * WIDE], v[:, 2 * WIDE :]
    y0, y1 = swap_y_hi(v0), swap_y_hi(rest)
    cut = [send_x(v_cut, 1), send_x(v_cut, -1), send_x(v_cut, 2)]
    cut = jnp.concatenate([v_cut, *cut], 0)
    y_cut = swap_y_hi(cut)
    t0 = turn(WIDE, 1280, v, other, y0, swap_core(y0), 0)
    y1_other = swap_core(y1)
    t1, t2 = [turn(s, w, v, other, y1, y1_other, s - 2 * WIDE) for s, w, _ in CHUNKS[1:]]
    near0 = [shift_x(t) for t in t0]
    o0 = shift_x(near0[0])
    near1 = [shift_x(t) for t in t1] if EARLY else None
    amps_in, cut, y_cut, near0, o0, near1, t1, t2 = lax.optimization_barrier((amps_in, cut, y_cut, near0, o0, near1, t1, t2))
    if not EARLY:
        near1 = [shift_x(t) for t in t1]
    amps = stack_amps(amps_in)
    near2 = [shift_x(t) for t in t2]
    o1 = shift_x(near1[0])
    o2 = shift_x(near2[0])
    work = [(t0, near0, o0), (t1, near1, o1), (t2, near2, o2)]
    out = None
    for j, (start, width, tile) in enumerate(CHUNKS):
        if j == CUT_AT:
            out = product_cut((cut, swap_core(cut), y_cut, swap_core(y_cut)), amps, shape, out)
        (f, s), (near_f, near_s), o = work[j]
        pieces = (f, swap_core(near_s), o, near_f, s, swap_core(near_f), swap_core(o), near_s)
        out = product(start, width, tile, pieces, amps, shape, out)
    return out


def solution(mesh):
    in_specs = (P("row", "col"), P("col", "row"))
    out_specs = P("row", "col")
    return jax.shard_map(body, mesh=mesh, in_specs=in_specs, out_specs=out_specs, check_vma=False)
```
